32 devices in a mesh: groups: 2 (over x), tensor: 16 (over z, y, core).
Axes of the slice: x: 2, y: 2, z: 4, core: 2. Of those that a mesh axis runs over, the one named last changes fastest.
Arguments:
- tokens: bfloat16 [64, 6144], P(('groups', 'tensor')), parts along dimension 0, may hold values from -6 to 6
- attn_gain: float32 [6144], replicated, may hold values from 0.25 to 1.75
- w_qkv: bfloat16 [6144, 8192], P(None, 'tensor'), may hold values from -4 to 4
- w_out: bfloat16 [6144, 6144], P(None, 'tensor'), may hold values from -0.078125 to 0.078125
- moe_gain: float32 [6144], replicated, may hold values from 0.25 to 1.75
- w_gate: bfloat16 [6144, 4096], P(None, 'tensor'), may hold values from -0.078125 to 0.078125
- w_up: bfloat16 [6144, 4096], P(None, 'tensor'), may hold values from -0.078125 to 0.078125
- w_down: bfloat16 [4096, 6144], P('tensor'), may hold values from -0.125 to 0.125
- expert_ids: int32 [64, 2], P(('groups', 'tensor')), parts along dimension 0, may hold values from 0 to 7, as said below
- gate_weights: float32 [64, 2], P(('groups', 'tensor')), parts along dimension 0, may hold values from 0.1 to 1
Outputs:
- layer_out: bfloat16 [64, 6144], P(('groups', 'tensor')), parts along dimension 0
The draws below stay inside these ranges and needn't reach their ends.
There are 2 independent parts, one for each index of `groups`. The reference program is written for one: setup_inputs(seed, part) draws one part's arguments, and reference() takes and returns one part's arrays. A program takes and returns all parts, laid end to end along the dimension named above; an argument that names none is the same for every part. Nothing has to cross between parts.
Inputs may be any that keep to these rules, and one draw needn't show every extreme that they name: `expert_ids`: each row names two different experts; in some aligned block of 2 rows every token names expert 0.
All inputs are finite; a program needn't handle non-finite values.
Results may differ from the reference program's by a relative error of at most 0.008.
Values may be sent and summed in bfloat16 or wider, within the bound.
A program may use at most 64 MiB of HBM per device.

```python
import math
import jax
import jax.numpy as jnp
from jax import lax

D = 6144
HEADS = 48
KV_HEADS = 8
HEAD_DIM = 128
EXPERT_COUNT = 8
EXPERT_WINDOW = 2
FF_DEV = 256
TOK_DEV = 2
SEQ = 32
QKV_W = 8192
ATT_W = 6144
FF_WIN = 2048
N_TENSOR = 16


def draw_expert_ids(key, part):
    key = jax.random.fold_in(key, 11)
    first_key, second_key = jax.random.split(key)
    router_scores = jax.random.randint(first_key, (SEQ, EXPERT_COUNT), 0, 1000)
    column_slot = jnp.arange(EXPERT_COUNT, dtype=jnp.int32)
    extra_logit = jnp.where(column_slot < EXPERT_WINDOW, 600, 0)
    blocks = SEQ // TOK_DEV
    chosen = jax.random.randint(second_key, (), 0, blocks)
    row_block = jnp.arange(SEQ, dtype=jnp.int32) // TOK_DEV
    forced_choice = jnp.where((row_block == chosen)[:, None] & (column_slot == 0)[None, :], 100000, 0)
    running_total = (router_scores + extra_logit[None, :] + forced_choice) * EXPERT_COUNT + column_slot[None, :]
    _, picked = lax.top_k(running_total, 2)
    return picked.astype(jnp.int32)


def draw_tokens(key, part):
    key = jax.random.fold_in(key, 21)
    noise_key = jax.random.fold_in(key, 0)
    drawn = jax.random.normal(noise_key, (SEQ, D), jnp.float32)
    return jnp.clip(drawn, -6.0, 6.0).astype(jnp.bfloat16)


def draw_w_qkv(key, part):
    key = jax.random.fold_in(key, 23)
    base_key = jax.random.fold_in(key, 0)
    drawn = jax.random.normal(base_key, (D, QKV_W), jnp.float32) / D ** 0.5
    return jnp.clip(drawn, -4.0, 4.0).astype(jnp.bfloat16)


def shard_levels(own_key, dims, cuts, low, largest):
    level, own = 1.0, jax.random.fold_in(own_key, 6)
    for dim, blocks in cuts:
        draws = jnp.exp(jax.random.uniform(jax.random.fold_in(own, dim), (blocks,), jnp.float32, low / len(cuts), largest / len(cuts)))
        level = level * jnp.repeat(draws, dims[dim] // blocks).reshape([-1 if axis == dim else 1 for axis in range(len(dims))])
    return level


def scatter_about(stream_key, extent, scale, most, cuts=(), kind=jnp.bfloat16):
    result = jax.random.normal(stream_key, extent, jnp.float32) * scale
    if len(cuts) > 0:
        result = shard_levels(stream_key, extent, cuts, -0.22, 0.18) * result
    return jnp.clip(result, min=-most, max=most).astype(kind)


def setup_inputs(seed: int = 0, part: int = 0) -> dict:
    key_list = jax.random.split(jax.random.key(seed), 11)
    part_keys = jax.random.split(jax.random.fold_in(key_list[10], part), 11)
    return {
        "tokens": draw_tokens(jax.random.fold_in(jax.random.fold_in(key_list[10], part), 71), part),
        "attn_gain": jnp.clip(1.0 + 0.15 * jax.random.normal(key_list[1], (D,), jnp.float32), 0.25, 1.75),
        "w_qkv": draw_w_qkv(jax.random.fold_in(key_list[10], 71), part),
        "w_out": scatter_about(key_list[3], (ATT_W, D), ATT_W ** -0.5, 0.078125, ((1, 16),)),
        "moe_gain": jnp.clip(1.0 + 0.15 * jax.random.normal(key_list[4], (D,), jnp.float32), 0.25, 1.75),
        "w_gate": scatter_about(key_list[5], (D, EXPERT_WINDOW * FF_WIN), D ** -0.5, 0.078125, ((1, 16),)),
        "w_up": scatter_about(key_list[6], (D, EXPERT_WINDOW * FF_WIN), D ** -0.5, 0.078125, ((1, 16),)),
        "w_down": scatter_about(key_list[7], (EXPERT_WINDOW * FF_WIN, D), FF_WIN ** -0.5, 0.125, ((0, 16),)),
        "expert_ids": draw_expert_ids(jax.random.fold_in(jax.random.fold_in(key_list[10], part), 71), part),
        "gate_weights": jnp.clip(jnp.exp(math.log(1.0) - 2.3025851 * jax.random.uniform(part_keys[9], (SEQ, 2), jnp.float32) ** shard_levels(part_keys[9], (SEQ, 2), ((0, 16),), -0.2, 0.2)), 0.1, 1.0),
    }


def rms_scale(values, gain):
    mean_square = lax.optimization_barrier(jnp.mean(values * values, axis=-1, keepdims=True))
    return values * lax.rsqrt(mean_square + 1e-05) * gain

def rotate(heads, positions):
    half = heads.shape[-1] // 2
    inverse = 1000000.0 ** (-(jnp.arange(half, dtype=jnp.float32) * 2.0) / heads.shape[-1])
    angles = positions[:, None] * inverse[None, :]
    cosine = jnp.cos(angles)[:, None, :]
    sine = jnp.sin(angles)[:, None, :]
    first = heads[..., :half]
    second = heads[..., half:]
    return jnp.concatenate([first * cosine - second * sine, second * cosine + first * sine], axis=-1)

def reference(tokens, attn_gain, w_qkv, w_out, moe_gain, w_gate, w_up, w_down, expert_ids, gate_weights):
    length = tokens.shape[0]
    group = HEADS // KV_HEADS
    kv_width = KV_HEADS * HEAD_DIM
    att_width = HEADS * HEAD_DIM
    tok_float = tokens.astype(jnp.float32)
    normed = rms_scale(tok_float, attn_gain).astype(jnp.bfloat16)
    qkv = jnp.dot(normed, w_qkv, preferred_element_type=jnp.float32).astype(jnp.bfloat16)
    positions = jnp.arange(length, dtype=jnp.float32)
    queries = qkv[:, :att_width].reshape(length, HEADS, HEAD_DIM).astype(jnp.float32)
    keys = qkv[:, att_width:att_width + kv_width].reshape(length, KV_HEADS, HEAD_DIM).astype(jnp.float32)
    values = qkv[:, att_width + kv_width:].reshape(length, KV_HEADS, HEAD_DIM)
    queries = rotate(queries, positions).astype(jnp.bfloat16)
    keys = rotate(keys, positions).astype(jnp.bfloat16)
    grouped = queries.reshape(length, KV_HEADS, group, HEAD_DIM).astype(jnp.float32)
    router_scores = jnp.einsum('qkgd,skd->kgqs', grouped, keys.astype(jnp.float32)) / jnp.sqrt(jnp.float32(HEAD_DIM))
    allowed = positions[None, :] <= positions[:, None]
    masked = jnp.where(allowed, router_scores, -jnp.inf)
    top = lax.optimization_barrier(jnp.max(masked, axis=-1, keepdims=True))
    weights = jnp.where(allowed, jnp.exp(masked - top), 0.0)
    running_total = lax.optimization_barrier(jnp.sum(weights, axis=-1))
    summed = jnp.einsum('kgqs,skd->kgqd', weights.astype(jnp.bfloat16).astype(jnp.float32), values.astype(jnp.float32))
    mixed = summed / running_total[..., None]
    mixed = jnp.transpose(mixed, (2, 0, 1, 3)).reshape(length, att_width).astype(jnp.bfloat16)
    attended = jnp.dot(mixed, w_out, preferred_element_type=jnp.float32).astype(jnp.bfloat16)
    residual = tok_float + attended.astype(jnp.float32)
    moe_in = rms_scale(residual, moe_gain).astype(jnp.bfloat16)
    owners = N_TENSOR // EXPERT_WINDOW
    combined = jnp.zeros((length, tokens.shape[1]), jnp.float32)
    for expert in range(EXPERT_WINDOW):
        lo = expert * FF_WIN
        gate_part = jnp.dot(moe_in, w_gate[:, lo:lo + FF_WIN], preferred_element_type=jnp.float32)
        up_part = jnp.dot(moe_in, w_up[:, lo:lo + FF_WIN], preferred_element_type=jnp.float32)
        hidden = (jax.nn.silu(gate_part) * up_part).astype(jnp.bfloat16)
        down_rows = w_down[lo:lo + FF_WIN]

        def add_block(index, total_sum):
            start = (index * FF_DEV).astype(jnp.int32)
            block = lax.dynamic_slice_in_dim(hidden, start, FF_DEV, 1)
            rows = lax.dynamic_slice_in_dim(down_rows, start, FF_DEV, 0)
            part = jnp.dot(block, rows, preferred_element_type=jnp.float32).astype(jnp.bfloat16)
            part = lax.optimization_barrier(part)
            return total_sum + part.astype(jnp.float32)
        expert_sum = lax.fori_loop(0, owners, add_block, jnp.zeros((length, tokens.shape[1]), jnp.float32))
        picked = lax.optimization_barrier(jnp.sum(jnp.where(expert_ids == expert, gate_weights, 0.0), axis=1))
        combined = combined + picked[:, None] * expert_sum
    return (residual + combined).astype(jnp.bfloat16)
```

```python
import functools

import jax
import jax.numpy as jnp
import numpy as np
from jax import lax
from jax.experimental import pallas as pl
from jax.experimental.pallas import tpu as pltpu
from jax.sharding import PartitionSpec as P

HEADS = 48
KV_HEADS = 8
GROUP = HEADS // KV_HEADS
HEAD_DIM = 128
EXPERT_WINDOW = 2
LANES = 128
CHUNK = 768
MESH = pl.DeviceIdType.MESH


def rotation_tables(size):
    half = HEAD_DIM // 2
    inverse = np.float32(1000000.0) ** (-(np.arange(half, dtype=np.float32) * 2.0) / HEAD_DIM)
    angles = np.arange(size, dtype=np.float32)[:, None] * inverse.astype(np.float32)[None, :]
    cosine, sine = np.cos(angles), np.sin(angles)
    return (
        np.concatenate([cosine, cosine], axis=1).astype(np.float32),
        np.concatenate([-sine, sine], axis=1).astype(np.float32),
    )


def rotate(head, cosine, sine):
    half = HEAD_DIM // 2
    swapped = jnp.concatenate([head[:, half:], head[:, :half]], axis=1)
    return head * cosine + swapped * sine


def kernel(
    n, tok_in, attn_gain_in, w_qkv_in, w_out_in, moe_gain_in, w_gate_in, w_up_in, w_down_in,
    cos_in, sin_in, ids, gates, out,
    w_qkv, w_out, w_gate, w_up, w_down, own_tok, attn_gain, moe_gain, cos_tab, sin_tab,
    stage, tok_all, tok_f32, x_all, columns, heads_out, k_buf, v_buf, mix_all, att_own, att_all,
    res_all, part_f32, part_all, part_in, small_sem, weight_sem, send_sem, recv_sem, kv_send, kv_recv,
):
    me = lax.axis_index("tensor")
    size = x_all.shape[1]
    width = x_all.shape[0] * CHUNK
    tiles = width // LANES
    rows = stage.shape[0] // tiles
    block = rows * tiles
    per_dev = w_qkv.shape[1] // HEAD_DIM
    q_devs = HEADS // per_dev
    kv_devs = KV_HEADS // per_dev
    chunks = width // CHUNK
    per_chunk = CHUNK // LANES
    out_cols = w_out.shape[1]

    small = [
        pltpu.make_async_copy(src, dst, small_sem.at[i])
        for i, (src, dst) in enumerate(
            [(tok_in, own_tok), (attn_gain_in, attn_gain), (moe_gain_in, moe_gain),
             (cos_in, cos_tab), (sin_in, sin_tab)]
        )
    ]
    weight = [
        pltpu.make_async_copy(src, dst, weight_sem.at[i])
        for i, (src, dst) in enumerate(
            [(w_qkv_in, w_qkv), (w_out_in, w_out), (w_gate_in, w_gate), (w_up_in, w_up),
             (w_down_in, w_down)]
        )
    ]
    for copy in small:
        copy.start()
    for copy in weight:
        copy.start()

    def peer(distance):
        return lax.rem(me + distance, n)

    barrier = pltpu.get_barrier_semaphore()

    @pl.loop(1, n)
    def _(distance):
        pl.semaphore_signal(
            barrier, inc=1, device_id={"tensor": peer(distance)}, device_id_type=MESH
        )

    small[0].wait()
    for tile in range(tiles):
        piece = own_tok[:, tile * LANES : (tile + 1) * LANES].astype(jnp.float32)
        for row in range(rows):
            stage[row * tiles + tile : row * tiles + tile + 1, :] = piece[row : row + 1, :]
    my_block = pl.ds(pl.multiple_of(me * block, 16), block)
    tok_all[my_block, :] = stage[...].astype(jnp.bfloat16)
    pl.semaphore_wait(barrier, n - 1)

    def remote(phase, src, dst, target):
        return pltpu.make_async_remote_copy(
            src_ref=src, dst_ref=dst, send_sem=send_sem.at[phase, target],
            recv_sem=recv_sem.at[phase, me], device_id={"tensor": target}, device_id_type=MESH,
        )

    def arrived(phase, source, dst):
        pltpu.make_async_remote_copy(
            src_ref=dst, dst_ref=dst, send_sem=send_sem.at[phase, source],
            recv_sem=recv_sem.at[phase, source], device_id={"tensor": source}, device_id_type=MESH,
        ).wait_recv()

    def token_block(ref, index):
        return ref.at[pl.ds(pl.multiple_of(index * block, 16), block), :]

    @pl.loop(1, n)
    def _(distance):
        remote(0, token_block(tok_all, me), token_block(tok_all, me), peer(distance)).start()

    @pl.loop(1, n)
    def _(distance):
        source = lax.rem(me + n - distance, n)
        arrived(0, source, token_block(tok_all, source))

    tok_f32[...] = tok_all[...].astype(jnp.float32)
    for copy in small[1:]:
        copy.wait()

    def tok_tile(tile):
        return tok_f32[pl.ds(tile, size, stride=tiles), :]

    def square_sum(chunk, total):
        for i in range(per_chunk):
            value = tok_tile(chunk * per_chunk + i)
            total = total + value * value
        return total

    total = lax.fori_loop(0, chunks, square_sum, jnp.zeros((size, LANES), jnp.float32))
    scale = lax.rsqrt(jnp.sum(total, axis=1, keepdims=True) / width + 1e-05)

    weight[0].wait()

    def project(chunk, total):
        pieces = []
        for i in range(per_chunk):
            tile = chunk * per_chunk + i
            pieces.append((tok_tile(tile) * scale * attn_gain[pl.ds(tile, 1), :]).astype(jnp.bfloat16))
        here = pl.ds(pl.multiple_of(chunk * CHUNK, CHUNK), CHUNK)
        return total + jnp.dot(
            jnp.concatenate(pieces, axis=1), w_qkv[here, :], preferred_element_type=jnp.float32
        )

    columns[...] = lax.fori_loop(
        0, chunks, project, jnp.zeros((size, w_qkv.shape[1]), jnp.float32)
    ).astype(jnp.bfloat16)

    is_query = me < q_devs
    is_key = jnp.logical_and(me >= q_devs, me < q_devs + kv_devs)
    is_value = me >= q_devs + kv_devs

    @pl.when(is_value)
    def _():
        for i in range(per_dev):
            heads_out[i] = columns[:, i * HEAD_DIM : (i + 1) * HEAD_DIM]

    @pl.when(jnp.logical_not(is_value))
    def _():
        for i in range(per_dev):
            head = columns[:, i * HEAD_DIM : (i + 1) * HEAD_DIM].astype(jnp.float32)
            heads_out[i] = rotate(head, cos_tab[...], sin_tab[...]).astype(jnp.bfloat16)

    fan = (GROUP - 2) // per_dev + 2

    def send_heads(first_dev, buf, kind, act):
        for i in range(per_dev):
            head = (me - first_dev) * per_dev + i
            for j in range(fan):
                target = (head * GROUP) // per_dev + j

                @pl.when(target <= (head * GROUP + GROUP - 1) // per_dev)
                def _():
                    slot = head - (target * per_dev) // GROUP
                    act(pltpu.make_async_remote_copy(
                        src_ref=heads_out.at[i], dst_ref=buf.at[slot],
                        send_sem=kv_send.at[i, j], recv_sem=kv_recv.at[kind, slot],
                        device_id={"tensor": target}, device_id_type=MESH,
                    ))

    @pl.when(is_key)
    def _():
        send_heads(q_devs, k_buf, 0, lambda copy: copy.start())

    @pl.when(is_value)
    def _():
        send_heads(q_devs + kv_devs, v_buf, 1, lambda copy: copy.start())

    @pl.when(is_query)
    def _():
        first = (me * per_dev) // GROUP
        last = (me * per_dev + per_dev - 1) // GROUP

        def kv_arrived(slot):
            for kind, buf in ((0, k_buf), (1, v_buf)):
                pltpu.make_async_remote_copy(
                    src_ref=buf.at[slot], dst_ref=buf.at[slot], send_sem=kv_send.at[0, 0],
                    recv_sem=kv_recv.at[kind, slot], device_id={"tensor": peer(1)}, device_id_type=MESH,
                ).wait_recv()

        kv_arrived(0)

        @pl.when(last > first)
        def _():
            kv_arrived(1)

        q_pos = lax.broadcasted_iota(jnp.int32, (size, size), 0)
        k_pos = lax.broadcasted_iota(jnp.int32, (size, size), 1)
        allowed = k_pos <= q_pos
        for i in range(per_dev):
            slot = (me * per_dev + i) // GROUP - first
            scores = lax.dot_general(
                heads_out[i], k_buf[slot], (((1,), (1,)), ((), ())),
                preferred_element_type=jnp.float32,
            ) * np.float32(1.0 / np.sqrt(HEAD_DIM))
            scores = jnp.where(allowed, scores, -1e30)
            top = jnp.max(scores, axis=1, keepdims=True)
            weights = jnp.where(allowed, jnp.exp(scores - top), 0.0)
            summed = jnp.dot(
                weights.astype(jnp.bfloat16), v_buf[slot], preferred_element_type=jnp.float32
            )
            mixed = summed / jnp.sum(weights, axis=1, keepdims=True)
            mix_all[me, :, i * HEAD_DIM : (i + 1) * HEAD_DIM] = mixed.astype(jnp.bfloat16)

        @pl.loop(1, n)
        def _(distance):
            remote(1, mix_all.at[me], mix_all.at[me], peer(distance)).start()

    @pl.loop(0, q_devs)
    def _(source):
        @pl.when(source != me)
        def _():
            arrived(1, source, mix_all.at[source])

    weight[1].wait()
    depth = w_qkv.shape[1]

    def out_project(source, total):
        here = pl.ds(pl.multiple_of(source * depth, depth), depth)
        return total + jnp.dot(
            mix_all[source], w_out[here, :], preferred_element_type=jnp.float32
        )

    att_own[...] = lax.fori_loop(
        0, q_devs, out_project, jnp.zeros((size, out_cols), jnp.float32)
    ).astype(jnp.bfloat16)
    att_all[me] = att_own[...]

    @pl.loop(1, n)
    def _(distance):
        remote(2, att_own, att_all.at[me], peer(distance)).start()

    @pl.loop(1, n)
    def _(distance):
        source = lax.rem(me + n - distance, n)
        arrived(2, source, att_all.at[source])

    per_att = CHUNK // out_cols

    def add_residual(chunk, total):
        attended = jnp.concatenate(
            [att_all[chunk * per_att + i].astype(jnp.float32) for i in range(per_att)], axis=1
        )
        for i in range(per_chunk):
            here = pl.ds(chunk * per_chunk + i, size, stride=tiles)
            value = tok_f32[here, :] + attended[:, i * LANES : (i + 1) * LANES]
            tok_f32[here, :] = value
            res_all[chunk, :, i * LANES : (i + 1) * LANES] = value
            total = total + value * value
        return total

    total = lax.fori_loop(0, chunks, add_residual, jnp.zeros((size, LANES), jnp.float32))
    scale2 = lax.rsqrt(jnp.sum(total, axis=1, keepdims=True) / width + 1e-05)
    weight[2].wait()
    weight[3].wait()

    def gate_up(chunk, totals):
        pieces = []
        for i in range(per_chunk):
            gain = moe_gain[pl.ds(chunk * per_chunk + i, 1), :]
            value = res_all[chunk, :, i * LANES : (i + 1) * LANES]
            pieces.append((value * scale2 * gain).astype(jnp.bfloat16))
        x = jnp.concatenate(pieces, axis=1)
        here = pl.ds(pl.multiple_of(chunk * CHUNK, CHUNK), CHUNK)
        return (
            totals[0] + jnp.dot(x, w_gate[here, :], preferred_element_type=jnp.float32),
            totals[1] + jnp.dot(x, w_up[here, :], preferred_element_type=jnp.float32),
        )

    zeros = jnp.zeros((size, w_gate.shape[1]), jnp.float32)
    gate, up = lax.fori_loop(0, chunks, gate_up, (zeros, zeros))
    hidden = (gate * (1.0 / (1.0 + jnp.exp(-gate))) * up).astype(jnp.bfloat16)
    weight[4].wait()

    @pl.loop(0, chunks)
    def _(chunk):
        here = pl.ds(pl.multiple_of(chunk * CHUNK, CHUNK), CHUNK)
        part = jnp.dot(hidden, w_down[:, here], preferred_element_type=jnp.float32)
        for i in range(per_chunk):
            part_f32[pl.ds(chunk * per_chunk + i, size, stride=tiles), :] = part[
                :, i * LANES : (i + 1) * LANES
            ]

    part_all[...] = part_f32[...].astype(jnp.bfloat16)

    @pl.loop(1, n)
    def _(distance):
        target = peer(distance)
        remote(3, token_block(part_all, target), part_in.at[me], target).start()

    part_in[me] = part_all[my_block, :]

    @pl.loop(1, n)
    def _(distance):
        source = lax.rem(me + n - distance, n)
        arrived(3, source, part_in.at[source])

    owners = n // EXPERT_WINDOW
    picked = [
        [
            sum(jnp.where(ids[row, k] == e, gates[row, k], 0.0) for k in range(2))
            for e in range(EXPERT_WINDOW)
        ]
        for row in range(rows)
    ]
    residual = tok_f32[my_block, :]
    for row in range(rows):
        total = residual[row * tiles : (row + 1) * tiles, :]
        for e in range(EXPERT_WINDOW):
            expert = lax.fori_loop(
                0, owners,
                lambda j, acc: acc + part_in[
                    e * owners + j, row * tiles : (row + 1) * tiles, :
                ].astype(jnp.float32),
                jnp.zeros((tiles, LANES), jnp.float32),
            )
            total = total + picked[row][e] * expert
        out[row * tiles : (row + 1) * tiles, :] = total.astype(jnp.bfloat16)

    @pl.when(is_key)
    def _():
        send_heads(q_devs, k_buf, 0, lambda copy: copy.wait_send())

    @pl.when(is_value)
    def _():
        send_heads(q_devs + kv_devs, v_buf, 1, lambda copy: copy.wait_send())

    @pl.loop(1, n)
    def _(distance):
        target = peer(distance)
        remote(0, token_block(tok_all, me), token_block(tok_all, me), target).wait_send()
        remote(2, att_own, att_all.at[me], target).wait_send()
        remote(3, token_block(part_all, target), part_in.at[me], target).wait_send()

        @pl.when(is_query)
        def _():
            remote(1, mix_all.at[me], mix_all.at[me], target).wait_send()


def on_device(
    tokens, attn_gain, w_qkv, w_out, moe_gain, w_gate, w_up, w_down, expert_ids, gate_weights
):
    n = lax.axis_size("tensor")
    rows, width = tokens.shape
    size = rows * n
    tiles = width // LANES
    block = rows * tiles
    per_dev = w_qkv.shape[1] // HEAD_DIM
    q_devs = HEADS // per_dev
    fan = (GROUP - 2) // per_dev + 2
    cosine, sine = rotation_tables(size)
    bf16, f32 = jnp.bfloat16, jnp.float32
    any_space = pl.BlockSpec(memory_space=pl.ANY)
    scalar_space = pl.BlockSpec(memory_space=pltpu.SMEM)
    result = pl.pallas_call(
        functools.partial(kernel, n),
        out_shape=jax.ShapeDtypeStruct((block, LANES), bf16),
        in_specs=[any_space] * 10 + [scalar_space] * 2,
        out_specs=pl.BlockSpec(memory_space=pltpu.VMEM),
        scratch_shapes=[
            pltpu.VMEM(w_qkv.shape, bf16),
            pltpu.VMEM(w_out.shape, bf16),
            pltpu.VMEM(w_gate.shape, bf16),
            pltpu.VMEM(w_up.shape, bf16),
            pltpu.VMEM(w_down.shape, bf16),
            pltpu.VMEM(tokens.shape, bf16),
            pltpu.VMEM((tiles, LANES), f32),
            pltpu.VMEM((tiles, LANES), f32),
            pltpu.VMEM((size, HEAD_DIM), f32),
            pltpu.VMEM((size, HEAD_DIM), f32),
            pltpu.VMEM((block, LANES), f32),
            pltpu.VMEM((n * block, LANES), bf16),
            pltpu.VMEM((n * block, LANES), f32),
            pltpu.VMEM((width // CHUNK, size, CHUNK), bf16),
            pltpu.VMEM((size, w_qkv.shape[1]), bf16),
            pltpu.VMEM((per_dev, size, HEAD_DIM), bf16),
            pltpu.VMEM((2, size, HEAD_DIM), bf16),
            pltpu.VMEM((2, size, HEAD_DIM), bf16),
            pltpu.VMEM((q_devs, size, w_qkv.shape[1]), bf16),
            pltpu.VMEM((size, w_out.shape[1]), bf16),
            pltpu.VMEM((n, size, w_out.shape[1]), bf16),
            pltpu.VMEM((width // CHUNK, size, CHUNK), f32),
            pltpu.VMEM((n * block, LANES), f32),
            pltpu.VMEM((n * block, LANES), bf16),
            pltpu.VMEM((n, block, LANES), bf16),
            pltpu.SemaphoreType.DMA((5,)),
            pltpu.SemaphoreType.DMA((5,)),
            pltpu.SemaphoreType.DMA((4, n)),
            pltpu.SemaphoreType.DMA((4, n)),
            pltpu.SemaphoreType.DMA((per_dev, fan)),
            pltpu.SemaphoreType.DMA((2, 2)),
        ],
        compiler_params=pltpu.CompilerParams(
            collective_id=0, has_side_effects=True, vmem_limit_bytes=56 * 1024 * 1024
        ),
        name="layer",
    )(
        tokens, attn_gain.reshape(tiles, LANES), w_qkv, w_out, moe_gain.reshape(tiles, LANES),
        w_gate, w_up, w_down, jnp.asarray(cosine), jnp.asarray(sine), expert_ids, gate_weights,
    )
    return result.reshape(rows, width)


def solution(mesh):
    return jax.shard_map(
        on_device,
        mesh=mesh,
        in_specs=(
            P(("groups", "tensor"), None),
            P(),
            P(None, "tensor"),
            P(None, "tensor"),
            P(),
            P(None, "tensor"),
            P(None, "tensor"),
            P("tensor", None),
            P(("groups", "tensor"), None),
            P(("groups", "tensor"), None),
        ),
        out_specs=P(("groups", "tensor"), None),
        check_vma=False,
    )
```

```python
import functools

import jax
import jax.numpy as jnp
import numpy as np
from jax import lax
from jax.experimental import pallas as pl
from jax.experimental.pallas import tpu as pltpu
from jax.sharding import PartitionSpec as P

HEADS = 48
KV_HEADS = 8
GROUP = HEADS // KV_HEADS
HEAD_DIM = 128
EXPERT_WINDOW = 2
LANES = 128
CHUNK = 768
MESH = pl.DeviceIdType.MESH


def rotation_tables(size):
    half = HEAD_DIM // 2
    inverse = np.float32(1000000.0) ** (-(np.arange(half, dtype=np.float32) * 2.0) / HEAD_DIM)
    angles = np.arange(size, dtype=np.float32)[:, None] * inverse.astype(np.float32)[None, :]
    cosine, sine = np.cos(angles), np.sin(angles)
    return (
        np.concatenate([cosine, cosine], axis=1).astype(np.float32),
        np.concatenate([-sine, sine], axis=1).astype(np.float32),
    )


def rotate(head, cosine, sine):
    half = HEAD_DIM // 2
    swapped = jnp.concatenate([head[:, half:], head[:, :half]], axis=1)
    return head * cosine + swapped * sine


def kernel(
    n, tok_in, attn_gain_in, w_qkv_in, w_out_in, moe_gain_in, w_gate_in, w_up_in, w_down_in,
    cos_in, sin_in, ids, gates, out,
    w_qkv, w_out, w_gate, w_up, w_down, own_tok, attn_gain, moe_gain, cos_tab, sin_tab,
    stage, tok_all, tok_f32, heads, att_all, gate_sum, up_sum, square_sum,
    part_f32, part_all, pair_in, pair_out, part_in,
    small_sem, weight_sem, send_sem, relay_sem, recv_sem, pair_sem,
):
    me = lax.axis_index("tensor")
    core = lax.rem(me, 2)
    chip = me // 2
    partner = me + 1 - 2 * core
    chips = n // 2
    size = gate_sum.shape[0]
    tiles = attn_gain.shape[0]
    width = tiles * LANES
    rows = stage.shape[0] // tiles
    block = rows * tiles
    per_dev = w_qkv.shape[1] // HEAD_DIM
    chunks = width // CHUNK
    per_chunk = CHUNK // LANES
    out_cols = w_out.shape[1]

    small = [
        pltpu.make_async_copy(src, dst, small_sem.at[i])
        for i, (src, dst) in enumerate(
            [(tok_in, own_tok), (attn_gain_in, attn_gain), (moe_gain_in, moe_gain),
             (cos_in, cos_tab), (sin_in, sin_tab)]
        )
    ]
    weight = [
        pltpu.make_async_copy(src, dst, weight_sem.at[i])
        for i, (src, dst) in enumerate(
            [(w_qkv_in, w_qkv), (w_out_in, w_out), (w_gate_in, w_gate), (w_up_in, w_up),
             (w_down_in, w_down)]
        )
    ]
    for copy in small:
        copy.start()
    for copy in weight:
        copy.start()

    def chip_at(step):
        z = lax.rem(chip // 2 + step // 2, chips // 2)
        return z * 2 + lax.rem(chip + step, 2)

    def chip_from(step):
        z = lax.rem(chip // 2 + chips // 2 - step // 2, chips // 2)
        return z * 2 + lax.rem(chip + step, 2)

    barrier = pltpu.get_barrier_semaphore()
    pl.semaphore_signal(barrier, inc=1, device_id={"tensor": partner}, device_id_type=MESH)

    @pl.loop(1, chips)
    def _(step):
        pl.semaphore_signal(
            barrier, inc=1, device_id={"tensor": chip_at(step) * 2 + core}, device_id_type=MESH
        )

    small[0].wait()
    for tile in range(tiles):
        piece = own_tok[:, tile * LANES : (tile + 1) * LANES].astype(jnp.float32)
        for row in range(rows):
            stage[row * tiles + tile : row * tiles + tile + 1, :] = piece[row : row + 1, :]
    tok_all[me] = stage[...].astype(jnp.bfloat16)
    my_block = pl.ds(pl.multiple_of(me * block, 16), block)
    tok_f32[my_block, :] = stage[...]
    pl.semaphore_wait(barrier, chips)

    def transfer(phase, src, dst, target, send, slot):
        return pltpu.make_async_remote_copy(
            src_ref=src, dst_ref=dst, send_sem=send, recv_sem=recv_sem.at[phase, slot],
            device_id={"tensor": target}, device_id_type=MESH,
        )

    def direct(phase, ref, step):
        return transfer(
            phase, ref.at[me], ref.at[me], chip_at(step) * 2 + core, send_sem.at[phase, step], me
        )

    def relay(phase, ref, step):
        source = chip_from(step) * 2 + core
        return transfer(
            phase, ref.at[source], ref.at[source], partner, relay_sem.at[phase, step], source
        )

    def arrived(phase, ref, source):
        transfer(
            phase, ref.at[source], ref.at[source], partner, relay_sem.at[phase, 0], source
        ).wait_recv()

    def gather(phase, ref, consume):
        @pl.loop(1, chips)
        def _(step):
            direct(phase, ref, chips - step).start()

        relay(phase, ref, 0).start()
        if consume is not None:
            consume(me)

        def take_direct(step):
            source = chip_from(step) * 2 + core
            arrived(phase, ref, source)
            relay(phase, ref, step).start()
            if consume is not None:
                consume(source)

        def take_relayed(step):
            source = chip_from(step) * 2 + 1 - core
            arrived(phase, ref, source)
            if consume is not None:
                consume(source)

        lag = min(4, chips)
        pl.loop(1, lag)(take_direct)

        @pl.loop(lag, chips)
        def _(step):
            take_direct(step)
            take_relayed(step - lag)

        pl.loop(chips - lag, chips)(take_relayed)

    def gather_left(phase, ref):
        @pl.loop(0, chips)
        def _(step):
            relay(phase, ref, step).wait_send()

        @pl.loop(1, chips)
        def _(step):
            direct(phase, ref, step).wait_send()

    def widen(source):
        here = pl.ds(pl.multiple_of(source * block, 16), block)
        tok_f32[here, :] = tok_all[source].astype(jnp.float32)

    gather(0, tok_all, widen)
    for copy in small[1:]:
        copy.wait()

    def tok_tile(tile):
        return tok_f32[pl.ds(tile, size, stride=tiles), :]

    def add_squares(chunk, total):
        for i in range(per_chunk):
            value = tok_tile(chunk * per_chunk + i)
            total = total + value * value
        return total

    total = lax.fori_loop(0, chunks, add_squares, jnp.zeros((size, LANES), jnp.float32))
    scale = lax.rsqrt(jnp.sum(total, axis=1, keepdims=True) / width + 1e-05)
    weight[0].wait()

    def project(chunk, total):
        pieces = []
        for i in range(per_chunk):
            tile = chunk * per_chunk + i
            pieces.append((tok_tile(tile) * scale * attn_gain[pl.ds(tile, 1), :]).astype(jnp.bfloat16))
        here = pl.ds(pl.multiple_of(chunk * CHUNK, CHUNK), CHUNK)
        return total + jnp.dot(
            jnp.concatenate(pieces, axis=1), w_qkv[here, :], preferred_element_type=jnp.float32
        )

    columns = lax.fori_loop(
        0, chunks, project, jnp.zeros((size, w_qkv.shape[1]), jnp.float32)
    ).astype(jnp.bfloat16)

    turns = jnp.where(me * per_dev >= HEADS + KV_HEADS, 0.0, 1.0)
    cosine = cos_tab[...] * turns + (1.0 - turns)
    sine = sin_tab[...] * turns
    for i in range(per_dev):
        head = columns[:, i * HEAD_DIM : (i + 1) * HEAD_DIM].astype(jnp.float32)
        heads[me, i] = rotate(head, cosine, sine).astype(jnp.bfloat16)

    gather(1, heads, None)
    weight[1].wait()

    q_pos = lax.rem(lax.broadcasted_iota(jnp.int32, (GROUP * size, size), 0), size)
    k_pos = lax.broadcasted_iota(jnp.int32, (GROUP * size, size), 1)
    allowed = k_pos <= q_pos

    def head_at(index):
        return heads[index // per_dev, lax.rem(index, per_dev)]

    def attend(g, total):
        queries = jnp.concatenate([head_at(g * GROUP + i) for i in range(GROUP)], axis=0)
        scores = lax.dot_general(
            queries, head_at(HEADS + g), (((1,), (1,)), ((), ())),
            preferred_element_type=jnp.float32,
        ) * np.float32(1.0 / np.sqrt(HEAD_DIM))
        scores = jnp.where(allowed, scores, -1e30)
        top = jnp.max(scores, axis=1, keepdims=True)
        weights = jnp.where(allowed, jnp.exp(scores - top), 0.0)
        summed = jnp.dot(
            weights.astype(jnp.bfloat16), head_at(HEADS + KV_HEADS + g),
            preferred_element_type=jnp.float32,
        )
        mixed = (summed / jnp.sum(weights, axis=1, keepdims=True)).astype(jnp.bfloat16)
        mixed = jnp.concatenate([mixed[i * size : (i + 1) * size] for i in range(GROUP)], axis=1)
        depth = GROUP * HEAD_DIM
        here = pl.ds(pl.multiple_of(g * depth, depth), depth)
        return total + jnp.dot(mixed, w_out[here, :], preferred_element_type=jnp.float32)

    att_all[me] = lax.fori_loop(
        0, KV_HEADS, attend, jnp.zeros((size, out_cols), jnp.float32)
    ).astype(jnp.bfloat16)

    gate_sum[...] = jnp.zeros_like(gate_sum)
    up_sum[...] = jnp.zeros_like(up_sum)
    square_sum[...] = jnp.zeros_like(square_sum)
    weight[2].wait()
    weight[3].wait()

    def expert_input(index, attended):
        wide = attended.shape[1]
        pieces = []
        total = square_sum[...]
        for i in range(wide // LANES):
            tile = index * (wide // LANES) + i
            here = pl.ds(tile, size, stride=tiles)
            value = tok_f32[here, :] + attended[:, i * LANES : (i + 1) * LANES]
            tok_f32[here, :] = value
            total = total + value * value
            pieces.append((value * moe_gain[pl.ds(tile, 1), :]).astype(jnp.bfloat16))
        square_sum[...] = total
        x = jnp.concatenate(pieces, axis=1)
        here = pl.ds(pl.multiple_of(index * wide, LANES), wide)
        gate_sum[...] += jnp.dot(x, w_gate[here, :], preferred_element_type=jnp.float32)
        up_sum[...] += jnp.dot(x, w_up[here, :], preferred_element_type=jnp.float32)

    if out_cols % LANES == 0:
        gather(2, att_all, lambda source: expert_input(source, att_all[source].astype(jnp.float32)))
    else:
        gather(2, att_all, None)
        joined = CHUNK // out_cols

        @pl.loop(0, chunks)
        def _(chunk):
            expert_input(chunk, jnp.concatenate(
                [att_all[chunk * joined + i].astype(jnp.float32) for i in range(joined)], axis=1
            ))

    scale = lax.rsqrt(jnp.sum(square_sum[...], axis=1, keepdims=True) / width + 1e-05)
    gate = gate_sum[...] * scale
    hidden = (gate * (1.0 / (1.0 + jnp.exp(-gate))) * (up_sum[...] * scale)).astype(jnp.bfloat16)
    weight[4].wait()

    @pl.loop(0, chunks)
    def _(chunk):
        here = pl.ds(pl.multiple_of(chunk * CHUNK, CHUNK), CHUNK)
        part = jnp.dot(hidden, w_down[:, here], preferred_element_type=jnp.float32)
        for i in range(per_chunk):
            part_f32[pl.ds(chunk * per_chunk + i, size, stride=tiles), :] = part[
                :, i * LANES : (i + 1) * LANES
            ]

    @pl.loop(0, n)
    def _(index):
        here = pl.ds(pl.multiple_of(index * block, 16), block)
        part_all[lax.rem(index, 2), index // 2] = part_f32[here, :].astype(jnp.bfloat16)

    pair = pltpu.make_async_remote_copy(
        src_ref=part_all.at[1 - core], dst_ref=pair_in, send_sem=pair_sem.at[0],
        recv_sem=pair_sem.at[1], device_id={"tensor": partner}, device_id_type=MESH,
    )
    pair.start()
    pair.wait_recv()

    def summed(index):
        return part_all[core, index].astype(jnp.float32) + pair_in[index].astype(jnp.float32)

    def deliver(step):
        target = chip_at(step)
        return transfer(
            3, pair_out.at[target], part_in.at[chip], target * 2 + core, send_sem.at[3, step], chip
        )

    @pl.loop(1, chips)
    def _(step):
        target = chip_at(chips - step)
        pair_out[target] = summed(target).astype(jnp.bfloat16)
        deliver(chips - step).start()

    part_in[chip] = summed(chip).astype(jnp.bfloat16)

    picked = [
        [
            sum(jnp.where(ids[row, k] == e, gates[row, k], 0.0) for k in range(2))
            for e in range(EXPERT_WINDOW)
        ]
        for row in range(rows)
    ]
    gather_left(0, tok_all)
    gather_left(1, heads)
    gather_left(2, att_all)
    pair.wait_send()

    @pl.loop(1, chips)
    def _(step):
        source = chip_from(step)
        transfer(
            3, part_in.at[source], part_in.at[source], partner, send_sem.at[3, 0], source
        ).wait_recv()

    owners = chips // EXPERT_WINDOW
    residual = tok_f32[my_block, :]
    for row in range(rows):
        total = residual[row * tiles : (row + 1) * tiles, :]
        for e in range(EXPERT_WINDOW):
            expert = jnp.zeros((tiles, LANES), jnp.float32)
            for j in range(owners):
                expert = expert + part_in[
                    e * owners + j, row * tiles : (row + 1) * tiles, :
                ].astype(jnp.float32)
            total = total + picked[row][e] * expert
        out[row * tiles : (row + 1) * tiles, :] = total.astype(jnp.bfloat16)

    @pl.loop(1, chips)
    def _(step):
        deliver(step).wait_send()


def on_device(
    tokens, attn_gain, w_qkv, w_out, moe_gain, w_gate, w_up, w_down, expert_ids, gate_weights
):
    n = lax.axis_size("tensor")
    rows, width = tokens.shape
    size = rows * n
    tiles = width // LANES
    block = rows * tiles
    per_dev = w_qkv.shape[1] // HEAD_DIM
    cosine, sine = rotation_tables(size)
    bf16, f32 = jnp.bfloat16, jnp.float32
    any_space = pl.BlockSpec(memory_space=pl.ANY)
    scalar_space = pl.BlockSpec(memory_space=pltpu.SMEM)
    result = pl.pallas_call(
        functools.partial(kernel, n),
        out_shape=jax.ShapeDtypeStruct((block, LANES), bf16),
        in_specs=[any_space] * 10 + [scalar_space] * 2,
        out_specs=pl.BlockSpec(memory_space=pltpu.VMEM),
        scratch_shapes=[
            pltpu.VMEM(w_qkv.shape, bf16),
            pltpu.VMEM(w_out.shape, bf16),
            pltpu.VMEM(w_gate.shape, bf16),
            pltpu.VMEM(w_up.shape, bf16),
            pltpu.VMEM(w_down.shape, bf16),
            pltpu.VMEM(tokens.shape, bf16),
            pltpu.VMEM((tiles, LANES), f32),
            pltpu.VMEM((tiles, LANES), f32),
            pltpu.VMEM((size, HEAD_DIM), f32),
            pltpu.VMEM((size, HEAD_DIM), f32),
            pltpu.VMEM((block, LANES), f32),
            pltpu.VMEM((n, block, LANES), bf16),
            pltpu.VMEM((n * block, LANES), f32),
            pltpu.VMEM((n, per_dev, size, HEAD_DIM), bf16),
            pltpu.VMEM((n, size, w_out.shape[1]), bf16),
            pltpu.VMEM((size, w_gate.shape[1]), f32),
            pltpu.VMEM((size, w_up.shape[1]), f32),
            pltpu.VMEM((size, LANES), f32),
            pltpu.VMEM((n * block, LANES), f32),
            pltpu.VMEM((2, n // 2, block, LANES), bf16),
            pltpu.VMEM((n // 2, block, LANES), bf16),
            pltpu.VMEM((n // 2, block, LANES), bf16),
            pltpu.VMEM((n // 2, block, LANES), bf16),
            pltpu.SemaphoreType.DMA((5,)),
            pltpu.SemaphoreType.DMA((5,)),
            pltpu.SemaphoreType.DMA((4, n // 2)),
            pltpu.SemaphoreType.DMA((3, n // 2)),
            pltpu.SemaphoreType.DMA((4, n)),
            pltpu.SemaphoreType.DMA((2,)),
        ],
        compiler_params=pltpu.CompilerParams(
            collective_id=0, has_side_effects=True, vmem_limit_bytes=56 * 1024 * 1024
        ),
        name="layer",
    )(
        tokens, attn_gain.reshape(tiles, LANES), w_qkv, w_out, moe_gain.reshape(tiles, LANES),
        w_gate, w_up, w_down, jnp.asarray(cosine), jnp.asarray(sine), expert_ids, gate_weights,
    )
    return result.reshape(rows, width)


def solution(mesh):
    return jax.shard_map(
        on_device,
        mesh=mesh,
        in_specs=(
            P(("groups", "tensor"), None),
            P(),
            P(None, "tensor"),
            P(None, "tensor"),
            P(),
            P(None, "tensor"),
            P(None, "tensor"),
            P("tensor", None),
            P(("groups", "tensor"), None),
            P(("groups", "tensor"), None),
        ),
        out_specs=P(("groups", "tensor"), None),
        check_vma=False,
    )
```

```python
import functools

import jax
import jax.numpy as jnp
import numpy as np
from jax import lax
from jax.experimental import pallas as pl
from jax.experimental.pallas import tpu as pltpu
from jax.sharding import PartitionSpec as P

HEADS = 48
KV_HEADS = 8
GROUP = HEADS // KV_HEADS
HEAD_DIM = 128
EXPERT_WINDOW = 2
LANES = 128
CHUNK = 768
MESH = pl.DeviceIdType.MESH


def rotation_tables(size):
    half = HEAD_DIM // 2
    inverse = np.float32(1000000.0) ** (-(np.arange(half, dtype=np.float32) * 2.0) / HEAD_DIM)
    angles = np.arange(size, dtype=np.float32)[:, None] * inverse.astype(np.float32)[None, :]
    cosine, sine = np.cos(angles), np.sin(angles)
    return (
        np.concatenate([cosine, cosine], axis=1).astype(np.float32),
        np.concatenate([-sine, sine], axis=1).astype(np.float32),
    )


def rotate(head, cosine, sine):
    half = HEAD_DIM // 2
    swapped = jnp.concatenate([head[:, half:], head[:, :half]], axis=1)
    return head * cosine + swapped * sine


def kernel(
    n, tok_in, attn_gain_in, w_qkv_in, w_out_in, moe_gain_in, w_gate_in, w_up_in, w_down_in,
    cos_in, sin_in, ids_in, gates_in, out,
    w_qkv, w_out, w_gate, w_up, w_down, own_tok, attn_gain, moe_gain, cos_tab, sin_tab,
    ids, gates, stage, tok_all, tok_f32, heads, att_all, gate_sum, up_sum, square_sum,
    part_f32, part_all, pair_in, pair_out, part_in,
    small_sem, weight_sem, send_sem, relay_sem, recv_sem, pair_sem,
):
    me = lax.axis_index("tensor")
    core = lax.rem(me, 2)
    chip = me // 2
    partner = me + 1 - 2 * core
    chips = n // 2
    size = gate_sum.shape[0]
    tiles = attn_gain.shape[0]
    width = tiles * LANES
    rows = stage.shape[0] // tiles
    block = rows * tiles
    per_dev = w_qkv.shape[1] // HEAD_DIM
    chunks = width // CHUNK
    per_chunk = CHUNK // LANES
    out_cols = w_out.shape[1]

    small = [
        pltpu.make_async_copy(src, dst, small_sem.at[i])
        for i, (src, dst) in enumerate(
            [(tok_in, own_tok), (attn_gain_in, attn_gain), (moe_gain_in, moe_gain),
             (cos_in, cos_tab), (sin_in, sin_tab), (ids_in, ids), (gates_in, gates)]
        )
    ]
    weight = [
        pltpu.make_async_copy(src, dst, weight_sem.at[i])
        for i, (src, dst) in enumerate(
            [(w_qkv_in, w_qkv), (w_out_in, w_out), (w_gate_in, w_gate), (w_up_in, w_up),
             (w_down_in, w_down)]
        )
    ]
    for copy in small:
        copy.start()
    for copy in weight:
        copy.start()

    def chip_at(step):
        z = lax.rem(chip // 2 + step // 2, chips // 2)
        return z * 2 + lax.rem(chip + step, 2)

    def chip_from(step):
        z = lax.rem(chip // 2 + chips // 2 - step // 2, chips // 2)
        return z * 2 + lax.rem(chip + step, 2)

    barrier = pltpu.get_barrier_semaphore()
    pl.semaphore_signal(barrier, inc=1, device_id={"tensor": partner}, device_id_type=MESH)

    @pl.loop(1, chips)
    def _(step):
        pl.semaphore_signal(
            barrier, inc=1, device_id={"tensor": chip_at(step) * 2 + core}, device_id_type=MESH
        )

    small[0].wait()
    for tile in range(tiles):
        piece = own_tok[:, tile * LANES : (tile + 1) * LANES].astype(jnp.float32)
        for row in range(rows):
            stage[row * tiles + tile : row * tiles + tile + 1, :] = piece[row : row + 1, :]
    tok_all[me] = stage[...].astype(jnp.bfloat16)
    my_block = pl.ds(pl.multiple_of(me * block, 16), block)
    tok_f32[my_block, :] = stage[...]
    pl.semaphore_wait(barrier, chips)

    def transfer(phase, src, dst, target, send, slot):
        return pltpu.make_async_remote_copy(
            src_ref=src, dst_ref=dst, send_sem=send, recv_sem=recv_sem.at[phase, slot],
            device_id={"tensor": target}, device_id_type=MESH,
        )

    def direct(phase, ref, step):
        return transfer(
            phase, ref.at[me], ref.at[me], chip_at(step) * 2 + core, send_sem.at[phase, step], me
        )

    def relay(phase, ref, step):
        source = chip_from(step) * 2 + core
        return transfer(
            phase, ref.at[source], ref.at[source], partner, relay_sem.at[phase, step], source
        )

    def arrived(phase, ref, source):
        transfer(
            phase, ref.at[source], ref.at[source], partner, relay_sem.at[phase, 0], source
        ).wait_recv()

    def gather(phase, ref, consume):
        @pl.loop(1, chips)
        def _(step):
            direct(phase, ref, chips - step).start()

        relay(phase, ref, 0).start()
        if consume is not None:
            consume(me)

        def take_direct(step):
            source = chip_from(step) * 2 + core
            arrived(phase, ref, source)
            relay(phase, ref, step).start()
            if consume is not None:
                consume(source)

        def take_relayed(step):
            source = chip_from(step) * 2 + 1 - core
            arrived(phase, ref, source)
            if consume is not None:
                consume(source)

        lag = min(4, chips)
        pl.loop(1, lag)(take_direct)

        @pl.loop(lag, chips)
        def _(step):
            take_direct(step)
            take_relayed(step - lag)

        pl.loop(chips - lag, chips)(take_relayed)

    def gather_left(phase, ref):
        @pl.loop(0, chips)
        def _(step):
            relay(phase, ref, step).wait_send()

        @pl.loop(1, chips)
        def _(step):
            direct(phase, ref, step).wait_send()

    def widen(source):
        here = pl.ds(pl.multiple_of(source * block, 16), block)
        tok_f32[here, :] = tok_all[source].astype(jnp.float32)

    gather(0, tok_all, widen)
    for copy in small[1:]:
        copy.wait()

    def tok_tile(tile):
        return tok_f32[pl.ds(tile, size, stride=tiles), :]

    weight[0].wait()

    def project(chunk, totals):
        product, squares = totals
        pieces = []
        for i in range(per_chunk):
            tile = chunk * per_chunk + i
            value = tok_tile(tile)
            squares = squares + value * value
            pieces.append((value * attn_gain[pl.ds(tile, 1), :]).astype(jnp.bfloat16))
        here = pl.ds(pl.multiple_of(chunk * CHUNK, CHUNK), CHUNK)
        x = jnp.concatenate(pieces, axis=1)
        return product + jnp.dot(x, w_qkv[here, :], preferred_element_type=jnp.float32), squares

    product, squares = lax.fori_loop(
        0, chunks, project,
        (jnp.zeros((size, w_qkv.shape[1]), jnp.float32), jnp.zeros((size, LANES), jnp.float32)),
    )
    scale = lax.rsqrt(jnp.sum(squares, axis=1, keepdims=True) / width + 1e-05)
    columns = (product * scale).astype(jnp.bfloat16)

    turns = jnp.where(me * per_dev >= HEADS + KV_HEADS, 0.0, 1.0)
    cosine = cos_tab[...] * turns + (1.0 - turns)
    sine = sin_tab[...] * turns
    for i in range(per_dev):
        head = columns[:, i * HEAD_DIM : (i + 1) * HEAD_DIM].astype(jnp.float32)
        heads[me, i] = rotate(head, cosine, sine).astype(jnp.bfloat16)

    gather(1, heads, None)
    weight[1].wait()

    q_pos = lax.rem(lax.broadcasted_iota(jnp.int32, (GROUP * size, size), 0), size)
    k_pos = lax.broadcasted_iota(jnp.int32, (GROUP * size, size), 1)
    allowed = k_pos <= q_pos

    def head_at(index):
        return heads[index // per_dev, lax.rem(index, per_dev)]

    def attend(g, total):
        queries = jnp.concatenate([head_at(g * GROUP + i) for i in range(GROUP)], axis=0)
        scores = lax.dot_general(
            queries, head_at(HEADS + g), (((1,), (1,)), ((), ())),
            preferred_element_type=jnp.float32,
        ) * np.float32(1.0 / np.sqrt(HEAD_DIM))
        scores = jnp.where(allowed, scores, -1e30)
        top = jnp.max(scores, axis=1, keepdims=True)
        weights = jnp.where(allowed, jnp.exp(scores - top), 0.0)
        summed = jnp.dot(
            weights.astype(jnp.bfloat16), head_at(HEADS + KV_HEADS + g),
            preferred_element_type=jnp.float32,
        )
        mixed = (summed / jnp.sum(weights, axis=1, keepdims=True)).astype(jnp.bfloat16)
        mixed = jnp.concatenate([mixed[i * size : (i + 1) * size] for i in range(GROUP)], axis=1)
        depth = GROUP * HEAD_DIM
        here = pl.ds(pl.multiple_of(g * depth, depth), depth)
        return total + jnp.dot(mixed, w_out[here, :], preferred_element_type=jnp.float32)

    att_all[me] = lax.fori_loop(
        0, KV_HEADS, attend, jnp.zeros((size, out_cols), jnp.float32), unroll=8
    ).astype(jnp.bfloat16)

    gate_sum[...] = jnp.zeros_like(gate_sum)
    up_sum[...] = jnp.zeros_like(up_sum)
    square_sum[...] = jnp.zeros_like(square_sum)
    weight[2].wait()
    weight[3].wait()

    def expert_input(index, attended):
        wide = attended.shape[1]
        pieces = []
        total = square_sum[...]
        for i in range(wide // LANES):
            tile = index * (wide // LANES) + i
            here = pl.ds(tile, size, stride=tiles)
            value = tok_f32[here, :] + attended[:, i * LANES : (i + 1) * LANES]
            tok_f32[here, :] = value
            total = total + value * value
            pieces.append((value * moe_gain[pl.ds(tile, 1), :]).astype(jnp.bfloat16))
        square_sum[...] = total
        x = jnp.concatenate(pieces, axis=1)
        here = pl.ds(pl.multiple_of(index * wide, LANES), wide)
        gate_sum[...] += jnp.dot(x, w_gate[here, :], preferred_element_type=jnp.float32)
        up_sum[...] += jnp.dot(x, w_up[here, :], preferred_element_type=jnp.float32)

    if out_cols % LANES == 0:
        gather(2, att_all, lambda source: expert_input(source, att_all[source].astype(jnp.float32)))
    else:
        gather(2, att_all, None)
        joined = CHUNK // out_cols

        @pl.loop(0, chunks)
        def _(chunk):
            expert_input(chunk, jnp.concatenate(
                [att_all[chunk * joined + i].astype(jnp.float32) for i in range(joined)], axis=1
            ))

    scale = lax.rsqrt(jnp.sum(square_sum[...], axis=1, keepdims=True) / width + 1e-05)
    gate = gate_sum[...] * scale
    hidden = (gate * (1.0 / (1.0 + jnp.exp(-gate))) * (up_sum[...] * scale)).astype(jnp.bfloat16)
    weight[4].wait()

    @pl.loop(0, chunks)
    def _(chunk):
        here = pl.ds(pl.multiple_of(chunk * CHUNK, CHUNK), CHUNK)
        part = jnp.dot(hidden, w_down[:, here], preferred_element_type=jnp.float32)
        for i in range(per_chunk):
            part_f32[pl.ds(chunk * per_chunk + i, size, stride=tiles), :] = part[
                :, i * LANES : (i + 1) * LANES
            ]

    @pl.loop(0, n)
    def _(index):
        here = pl.ds(pl.multiple_of(index * block, 16), block)
        part_all[lax.rem(index, 2), index // 2] = part_f32[here, :].astype(jnp.bfloat16)

    pair = pltpu.make_async_remote_copy(
        src_ref=part_all.at[1 - core], dst_ref=pair_in, send_sem=pair_sem.at[0],
        recv_sem=pair_sem.at[1], device_id={"tensor": partner}, device_id_type=MESH,
    )
    pair.start()
    pair.wait_recv()

    def summed(index):
        return part_all[core, index].astype(jnp.float32) + pair_in[index].astype(jnp.float32)

    def deliver(step):
        target = chip_at(step)
        return transfer(
            3, pair_out.at[target], part_in.at[chip], target * 2 + core, send_sem.at[3, step], chip
        )

    @pl.loop(1, chips)
    def _(step):
        target = chip_at(chips - step)
        pair_out[target] = summed(target).astype(jnp.bfloat16)
        deliver(chips - step).start()

    part_in[chip] = summed(chip).astype(jnp.bfloat16)

    picked = [
        [
            sum(jnp.where(ids[row, k] == e, gates[row, k], 0.0) for k in range(2))
            for e in range(EXPERT_WINDOW)
        ]
        for row in range(rows)
    ]
    gather_left(0, tok_all)
    gather_left(1, heads)
    gather_left(2, att_all)
    pair.wait_send()

    @pl.loop(1, chips)
    def _(step):
        source = chip_from(step)
        transfer(
            3, part_in.at[source], part_in.at[source], partner, send_sem.at[3, 0], source
        ).wait_recv()

    owners = chips // EXPERT_WINDOW
    residual = tok_f32[my_block, :]
    for row in range(rows):
        total = residual[row * tiles : (row + 1) * tiles, :]
        for e in range(EXPERT_WINDOW):
            expert = jnp.zeros((tiles, LANES), jnp.float32)
            for j in range(owners):
                expert = expert + part_in[
                    e * owners + j, row * tiles : (row + 1) * tiles, :
                ].astype(jnp.float32)
            total = total + picked[row][e] * expert
        stage[row * tiles : (row + 1) * tiles, :] = total
    for tile in range(tiles):
        out[:, tile * LANES : (tile + 1) * LANES] = stage[
            pl.ds(tile, rows, stride=tiles), :
        ].astype(jnp.bfloat16)

    @pl.loop(1, chips)
    def _(step):
        deliver(step).wait_send()


def on_device(
    tokens, attn_gain, w_qkv, w_out, moe_gain, w_gate, w_up, w_down, expert_ids, gate_weights
):
    n = lax.axis_size("tensor")
    rows, width = tokens.shape
    size = rows * n
    tiles = width // LANES
    block = rows * tiles
    per_dev = w_qkv.shape[1] // HEAD_DIM
    cosine, sine = rotation_tables(size)
    bf16, f32 = jnp.bfloat16, jnp.float32
    any_space = pl.BlockSpec(memory_space=pl.ANY)
    result = pl.pallas_call(
        functools.partial(kernel, n),
        out_shape=jax.ShapeDtypeStruct((rows, width), bf16),
        in_specs=[any_space] * 12,
        out_specs=pl.BlockSpec(memory_space=pltpu.VMEM),
        scratch_shapes=[
            pltpu.VMEM(w_qkv.shape, bf16),
            pltpu.VMEM(w_out.shape, bf16),
            pltpu.VMEM(w_gate.shape, bf16),
            pltpu.VMEM(w_up.shape, bf16),
            pltpu.VMEM(w_down.shape, bf16),
            pltpu.VMEM(tokens.shape, bf16),
            pltpu.VMEM((tiles, LANES), f32),
            pltpu.VMEM((tiles, LANES), f32),
            pltpu.VMEM((size, HEAD_DIM), f32),
            pltpu.VMEM((size, HEAD_DIM), f32),
            pltpu.SMEM(expert_ids.shape, jnp.int32),
            pltpu.SMEM(gate_weights.shape, f32),
            pltpu.VMEM((block, LANES), f32),
            pltpu.VMEM((n, block, LANES), bf16),
            pltpu.VMEM((n * block, LANES), f32),
            pltpu.VMEM((n, per_dev, size, HEAD_DIM), bf16),
            pltpu.VMEM((n, size, w_out.shape[1]), bf16),
            pltpu.VMEM((size, w_gate.shape[1]), f32),
            pltpu.VMEM((size, w_up.shape[1]), f32),
            pltpu.VMEM((size, LANES), f32),
            pltpu.VMEM((n * block, LANES), f32),
            pltpu.VMEM((2, n // 2, block, LANES), bf16),
            pltpu.VMEM((n // 2, block, LANES), bf16),
            pltpu.VMEM((n // 2, block, LANES), bf16),
            pltpu.VMEM((n // 2, block, LANES), bf16),
            pltpu.SemaphoreType.DMA((7,)),
            pltpu.SemaphoreType.DMA((5,)),
            pltpu.SemaphoreType.DMA((4, n // 2)),
            pltpu.SemaphoreType.DMA((3, n // 2)),
            pltpu.SemaphoreType.DMA((4, n)),
            pltpu.SemaphoreType.DMA((2,)),
        ],
        compiler_params=pltpu.CompilerParams(
            collective_id=0, has_side_effects=True, vmem_limit_bytes=56 * 1024 * 1024
        ),
        name="layer",
    )(
        tokens, attn_gain.reshape(tiles, LANES), w_qkv, w_out, moe_gain.reshape(tiles, LANES),
        w_gate, w_up, w_down, jnp.asarray(cosine), jnp.asarray(sine), expert_ids, gate_weights,
    )
    return result


def solution(mesh):
    return jax.shard_map(
        on_device,
        mesh=mesh,
        in_specs=(
            P(("groups", "tensor"), None),
            P(),
            P(None, "tensor"),
            P(None, "tensor"),
            P(),
            P(None, "tensor"),
            P(None, "tensor"),
            P("tensor", None),
            P(("groups", "tensor"), None),
            P(("groups", "tensor"), None),
        ),
        out_specs=P(("groups", "tensor"), None),
        check_vma=False,
    )
```

```python
import functools

import jax
import jax.numpy as jnp
import numpy as np
from jax import lax
from jax.experimental import pallas as pl
from jax.experimental.pallas import tpu as pltpu
from jax.sharding import PartitionSpec as P

HEADS = 48
KV_HEADS = 8
GROUP = HEADS // KV_HEADS
HEAD_DIM = 128
EXPERT_WINDOW = 2
LANES = 128
CHUNK = 768
PIECE = 16
MESH = pl.DeviceIdType.MESH


def rotation_tables(size):
    half = HEAD_DIM // 2
    inverse = np.float32(1000000.0) ** (-(np.arange(half, dtype=np.float32) * 2.0) / HEAD_DIM)
    angles = np.arange(size, dtype=np.float32)[:, None] * inverse.astype(np.float32)[None, :]
    cosine, sine = np.cos(angles), np.sin(angles)
    return (
        np.concatenate([cosine, cosine], axis=1).astype(np.float32),
        np.concatenate([-sine, sine], axis=1).astype(np.float32),
    )


def rotate(head, cosine, sine):
    half = HEAD_DIM // 2
    swapped = jnp.concatenate([head[:, half:], head[:, :half]], axis=1)
    return head * cosine + swapped * sine


def kernel(
    n, tok_in, attn_gain_in, w_qkv_in, w_out_in, moe_gain_in, w_gate_in, w_up_in, w_down_in,
    cos_in, sin_in, ids_in, gates_in, out,
    w_qkv, w_out, w_gate, w_up, w_down, own_tok, attn_gain, moe_gain, cos_tab, sin_tab,
    ids, gates, stage, tok_all, tok_f32, heads, att_all, gate_sum, up_sum, square_sum,
    part_f32, part_all, pair_in, pair_out, part_in,
    small_sem, weight_sem, send_sem, relay_sem, recv_sem, pair_sem, out_send, out_recv,
):
    me = lax.axis_index("tensor")
    core = lax.rem(me, 2)
    chip = me // 2
    partner = me + 1 - 2 * core
    chips = n // 2
    size = gate_sum.shape[0]
    tiles = attn_gain.shape[0]
    width = tiles * LANES
    rows = stage.shape[0] // tiles
    block = rows * tiles
    per_dev = w_qkv.shape[1] // HEAD_DIM
    chunks = width // CHUNK
    per_chunk = CHUNK // LANES
    out_cols = w_out.shape[1]
    pieces = tiles // PIECE
    share = rows * PIECE

    small = [
        pltpu.make_async_copy(src, dst, small_sem.at[i])
        for i, (src, dst) in enumerate(
            [(tok_in, own_tok), (attn_gain_in, attn_gain), (moe_gain_in, moe_gain),
             (cos_in, cos_tab), (sin_in, sin_tab), (ids_in, ids), (gates_in, gates)]
        )
    ]
    weight = [
        pltpu.make_async_copy(src, dst, weight_sem.at[i])
        for i, (src, dst) in enumerate(
            [(w_qkv_in, w_qkv), (w_out_in, w_out), (w_gate_in, w_gate), (w_up_in, w_up),
             (w_down_in, w_down)]
        )
    ]
    for copy in small:
        copy.start()
    for copy in weight:
        copy.start()

    def chip_at(step):
        bits = [2**b for b in range(chips.bit_length() - 1)]
        return sum(lax.rem(chip // bit + step // bit, 2) * bit for bit in bits)

    chip_from = chip_at

    barrier = pltpu.get_barrier_semaphore()
    pl.semaphore_signal(barrier, inc=1, device_id={"tensor": partner}, device_id_type=MESH)

    @pl.loop(1, chips)
    def _(step):
        pl.semaphore_signal(
            barrier, inc=1, device_id={"tensor": chip_at(step) * 2 + core}, device_id_type=MESH
        )

    small[0].wait()
    for tile in range(tiles):
        piece = own_tok[:, tile * LANES : (tile + 1) * LANES].astype(jnp.float32)
        for row in range(rows):
            stage[row * tiles + tile : row * tiles + tile + 1, :] = piece[row : row + 1, :]
    tok_all[me] = stage[...].astype(jnp.bfloat16)
    my_block = pl.ds(pl.multiple_of(me * block, 16), block)
    tok_f32[my_block, :] = stage[...]
    pl.semaphore_wait(barrier, chips)

    def transfer(phase, src, dst, target, send, slot):
        return pltpu.make_async_remote_copy(
            src_ref=src, dst_ref=dst, send_sem=send, recv_sem=recv_sem.at[phase, slot],
            device_id={"tensor": target}, device_id_type=MESH,
        )

    def direct(phase, ref, step):
        return transfer(
            phase, ref.at[me], ref.at[me], chip_at(step) * 2 + core, send_sem.at[phase, step], me
        )

    def relay(phase, ref, step):
        source = chip_from(step) * 2 + core
        return transfer(
            phase, ref.at[source], ref.at[source], partner, relay_sem.at[phase, step], source
        )

    def arrived(phase, ref, source):
        transfer(
            phase, ref.at[source], ref.at[source], partner, relay_sem.at[phase, 0], source
        ).wait_recv()

    def gather(phase, ref, consume):
        @pl.loop(1, chips)
        def _(step):
            direct(phase, ref, chips - step).start()

        relay(phase, ref, 0).start()
        if consume is not None:
            consume(me)

        def take_direct(step):
            source = chip_from(step) * 2 + core
            arrived(phase, ref, source)
            relay(phase, ref, step).start()
            if consume is not None:
                consume(source)

        def take_relayed(step):
            source = chip_from(step) * 2 + 1 - core
            arrived(phase, ref, source)
            if consume is not None:
                consume(source)

        lag = min(4, chips)
        pl.loop(1, lag)(take_direct)

        @pl.loop(lag, chips)
        def _(step):
            take_direct(step)
            take_relayed(step - lag)

        pl.loop(chips - lag, chips)(take_relayed)

    def gather_left(phase, ref):
        @pl.loop(0, chips)
        def _(step):
            relay(phase, ref, step).wait_send()

        @pl.loop(1, chips)
        def _(step):
            direct(phase, ref, step).wait_send()

    def widen(source):
        here = pl.ds(pl.multiple_of(source * block, 16), block)
        tok_f32[here, :] = tok_all[source].astype(jnp.float32)

    gather(0, tok_all, widen)
    for copy in small[1:]:
        copy.wait()

    def tok_tile(tile):
        return tok_f32[pl.ds(tile, size, stride=tiles), :]

    weight[0].wait()

    def project(chunk, totals):
        product, squares = totals
        pieces = []
        for i in range(per_chunk):
            tile = chunk * per_chunk + i
            value = tok_tile(tile)
            squares = squares + value * value
            pieces.append((value * attn_gain[pl.ds(tile, 1), :]).astype(jnp.bfloat16))
        here = pl.ds(pl.multiple_of(chunk * CHUNK, CHUNK), CHUNK)
        x = jnp.concatenate(pieces, axis=1)
        return product + jnp.dot(x, w_qkv[here, :], preferred_element_type=jnp.float32), squares

    product, squares = lax.fori_loop(
        0, chunks, project,
        (jnp.zeros((size, w_qkv.shape[1]), jnp.float32), jnp.zeros((size, LANES), jnp.float32)),
    )
    scale = lax.rsqrt(jnp.sum(squares, axis=1, keepdims=True) / width + 1e-05)
    columns = (product * scale).astype(jnp.bfloat16)

    turns = jnp.where(me * per_dev >= HEADS + KV_HEADS, 0.0, 1.0)
    cosine = cos_tab[...] * turns + (1.0 - turns)
    sine = sin_tab[...] * turns
    for i in range(per_dev):
        head = columns[:, i * HEAD_DIM : (i + 1) * HEAD_DIM].astype(jnp.float32)
        heads[me, i] = rotate(head, cosine, sine).astype(jnp.bfloat16)

    gather(1, heads, None)
    weight[1].wait()

    q_pos = lax.rem(lax.broadcasted_iota(jnp.int32, (GROUP * size, size), 0), size)
    k_pos = lax.broadcasted_iota(jnp.int32, (GROUP * size, size), 1)
    allowed = k_pos <= q_pos

    def head_at(index):
        return heads[index // per_dev, lax.rem(index, per_dev)]

    def attend(g, total):
        queries = jnp.concatenate([head_at(g * GROUP + i) for i in range(GROUP)], axis=0)
        scores = lax.dot_general(
            queries, head_at(HEADS + g), (((1,), (1,)), ((), ())),
            preferred_element_type=jnp.float32,
        ) * np.float32(1.0 / np.sqrt(HEAD_DIM))
        scores = jnp.where(allowed, scores, -1e30)
        top = jnp.max(scores, axis=1, keepdims=True)
        weights = jnp.where(allowed, jnp.exp(scores - top), 0.0)
        summed = jnp.dot(
            weights.astype(jnp.bfloat16), head_at(HEADS + KV_HEADS + g),
            preferred_element_type=jnp.float32,
        )
        mixed = (summed / jnp.sum(weights, axis=1, keepdims=True)).astype(jnp.bfloat16)
        mixed = jnp.concatenate([mixed[i * size : (i + 1) * size] for i in range(GROUP)], axis=1)
        depth = GROUP * HEAD_DIM
        here = pl.ds(pl.multiple_of(g * depth, depth), depth)
        return total + jnp.dot(mixed, w_out[here, :], preferred_element_type=jnp.float32)

    att_all[me] = lax.fori_loop(
        0, KV_HEADS, attend, jnp.zeros((size, out_cols), jnp.float32), unroll=8
    ).astype(jnp.bfloat16)

    gate_sum[...] = jnp.zeros_like(gate_sum)
    up_sum[...] = jnp.zeros_like(up_sum)
    square_sum[...] = jnp.zeros_like(square_sum)
    weight[2].wait()
    weight[3].wait()

    def expert_input(index, attended):
        wide = attended.shape[1]
        pieces = []
        total = square_sum[...]
        for i in range(wide // LANES):
            tile = index * (wide // LANES) + i
            here = pl.ds(tile, size, stride=tiles)
            value = tok_f32[here, :] + attended[:, i * LANES : (i + 1) * LANES]
            tok_f32[here, :] = value
            total = total + value * value
            pieces.append((value * moe_gain[pl.ds(tile, 1), :]).astype(jnp.bfloat16))
        square_sum[...] = total
        x = jnp.concatenate(pieces, axis=1)
        here = pl.ds(pl.multiple_of(index * wide, LANES), wide)
        gate_sum[...] += jnp.dot(x, w_gate[here, :], preferred_element_type=jnp.float32)
        up_sum[...] += jnp.dot(x, w_up[here, :], preferred_element_type=jnp.float32)

    if out_cols % LANES == 0:
        gather(2, att_all, lambda source: expert_input(source, att_all[source].astype(jnp.float32)))
    else:
        gather(2, att_all, None)
        joined = CHUNK // out_cols

        @pl.loop(0, chunks)
        def _(chunk):
            expert_input(chunk, jnp.concatenate(
                [att_all[chunk * joined + i].astype(jnp.float32) for i in range(joined)], axis=1
            ))

    scale = lax.rsqrt(jnp.sum(square_sum[...], axis=1, keepdims=True) / width + 1e-05)
    gate = gate_sum[...] * scale
    hidden = (gate * (1.0 / (1.0 + jnp.exp(-gate))) * (up_sum[...] * scale)).astype(jnp.bfloat16)
    weight[4].wait()

    def pair(piece):
        return pltpu.make_async_remote_copy(
            src_ref=part_all.at[piece, 1 - core], dst_ref=pair_in.at[piece],
            send_sem=pair_sem.at[0, piece], recv_sem=pair_sem.at[1, piece],
            device_id={"tensor": partner}, device_id_type=MESH,
        )

    def summed(piece, index):
        return (
            part_all[piece, core, index].astype(jnp.float32)
            + pair_in[piece, index].astype(jnp.float32)
        )

    def delivery(piece, target, slot, step):
        return pltpu.make_async_remote_copy(
            src_ref=pair_out.at[piece, target], dst_ref=part_in.at[piece, slot],
            send_sem=out_send.at[piece, step], recv_sem=out_recv.at[piece, slot],
            device_id={"tensor": target * 2 + core}, device_id_type=MESH,
        )

    strip = 4 * LANES
    for piece in range(pieces):
        for j in range(PIECE * LANES // strip):
            first = piece * PIECE * LANES + j * strip
            part = jnp.dot(
                hidden, w_down[:, first : first + strip], preferred_element_type=jnp.float32
            )
            for i in range(strip // LANES):
                part_f32[piece, pl.ds(j * (strip // LANES) + i, size, stride=PIECE), :] = part[
                    :, i * LANES : (i + 1) * LANES
                ]

        @pl.loop(0, chips, unroll=4)
        def _(index):
            for c in range(2):
                here = pl.ds(pl.multiple_of((index * 2 + c) * share, 16), share)
                part_all[piece, c, index] = part_f32[piece, here, :].astype(jnp.bfloat16)

        pair(piece).start()

    for piece in range(pieces):
        pair(piece).wait_recv()

        @pl.loop(1, chips)
        def _(step):
            target = chip_at(chips - step)
            pair_out[piece, target] = summed(piece, target).astype(jnp.bfloat16)
            delivery(piece, target, chip, chips - step).start()

        part_in[piece, chip] = summed(piece, chip).astype(jnp.bfloat16)

    picked = [
        [
            sum(jnp.where(ids[row, k] == e, gates[row, k], 0.0) for k in range(2))
            for e in range(EXPERT_WINDOW)
        ]
        for row in range(rows)
    ]
    gather_left(0, tok_all)
    gather_left(1, heads)
    gather_left(2, att_all)
    owners = chips // EXPERT_WINDOW
    for piece in range(pieces):
        pair(piece).wait_send()

        @pl.loop(1, chips)
        def _(step):
            delivery(piece, chip, chip_from(step), step).wait_recv()

        for row in range(rows):
            first = row * tiles + piece * PIECE
            total = tok_f32[pl.ds(pl.multiple_of(me * block + first, 8), PIECE), :]
            for e in range(EXPERT_WINDOW):
                expert = jnp.zeros((PIECE, LANES), jnp.float32)
                for j in range(owners):
                    expert = expert + part_in[
                        piece, e * owners + j, row * PIECE : (row + 1) * PIECE, :
                    ].astype(jnp.float32)
                total = total + picked[row][e] * expert
            stage[first : first + PIECE, :] = total

    for tile in range(tiles):
        out[:, tile * LANES : (tile + 1) * LANES] = stage[
            pl.ds(tile, rows, stride=tiles), :
        ].astype(jnp.bfloat16)

    for piece in range(pieces):
        @pl.loop(1, chips)
        def _(step):
            delivery(piece, chip_at(step), chip, step).wait_send()


def on_device(
    tokens, attn_gain, w_qkv, w_out, moe_gain, w_gate, w_up, w_down, expert_ids, gate_weights
):
    n = lax.axis_size("tensor")
    rows, width = tokens.shape
    size = rows * n
    tiles = width // LANES
    block = rows * tiles
    per_dev = w_qkv.shape[1] // HEAD_DIM
    pieces = tiles // PIECE
    share = rows * PIECE
    cosine, sine = rotation_tables(size)
    bf16, f32 = jnp.bfloat16, jnp.float32
    any_space = pl.BlockSpec(memory_space=pl.ANY)
    result = pl.pallas_call(
        functools.partial(kernel, n),
        out_shape=jax.ShapeDtypeStruct((rows, width), bf16),
        in_specs=[any_space] * 12,
        out_specs=pl.BlockSpec(memory_space=pltpu.VMEM),
        scratch_shapes=[
            pltpu.VMEM(w_qkv.shape, bf16),
            pltpu.VMEM(w_out.shape, bf16),
            pltpu.VMEM(w_gate.shape, bf16),
            pltpu.VMEM(w_up.shape, bf16),
            pltpu.VMEM(w_down.shape, bf16),
            pltpu.VMEM(tokens.shape, bf16),
            pltpu.VMEM((tiles, LANES), f32),
            pltpu.VMEM((tiles, LANES), f32),
            pltpu.VMEM((size, HEAD_DIM), f32),
            pltpu.VMEM((size, HEAD_DIM), f32),
            pltpu.SMEM(expert_ids.shape, jnp.int32),
            pltpu.SMEM(gate_weights.shape, f32),
            pltpu.VMEM((block, LANES), f32),
            pltpu.VMEM((n, block, LANES), bf16),
            pltpu.VMEM((n * block, LANES), f32),
            pltpu.VMEM((n, per_dev, size, HEAD_DIM), bf16),
            pltpu.VMEM((n, size, w_out.shape[1]), bf16),
            pltpu.VMEM((size, w_gate.shape[1]), f32),
            pltpu.VMEM((size, w_up.shape[1]), f32),
            pltpu.VMEM((size, LANES), f32),
            pltpu.VMEM((pieces, n * share, LANES), f32),
            pltpu.VMEM((pieces, 2, n // 2, share, LANES), bf16),
            pltpu.VMEM((pieces, n // 2, share, LANES), bf16),
            pltpu.VMEM((pieces, n // 2, share, LANES), bf16),
            pltpu.VMEM((pieces, n // 2, share, LANES), bf16),
            pltpu.SemaphoreType.DMA((7,)),
            pltpu.SemaphoreType.DMA((5,)),
            pltpu.SemaphoreType.DMA((3, n // 2)),
            pltpu.SemaphoreType.DMA((3, n // 2)),
            pltpu.SemaphoreType.DMA((3, n)),
            pltpu.SemaphoreType.DMA((2, pieces)),
            pltpu.SemaphoreType.DMA((pieces, n // 2)),
            pltpu.SemaphoreType.DMA((pieces, n // 2)),
        ],
        compiler_params=pltpu.CompilerParams(
            collective_id=0, has_side_effects=True, vmem_limit_bytes=56 * 1024 * 1024
        ),
        name="layer",
    )(
        tokens, attn_gain.reshape(tiles, LANES), w_qkv, w_out, moe_gain.reshape(tiles, LANES),
        w_gate, w_up, w_down, jnp.asarray(cosine), jnp.asarray(sine), expert_ids, gate_weights,
    )
    return result


def solution(mesh):
    return jax.shard_map(
        on_device,
        mesh=mesh,
        in_specs=(
            P(("groups", "tensor"), None),
            P(),
            P(None, "tensor"),
            P(None, "tensor"),
            P(),
            P(None, "tensor"),
            P(None, "tensor"),
            P("tensor", None),
            P(("groups", "tensor"), None),
            P(("groups", "tensor"), None),
        ),
        out_specs=P(("groups", "tensor"), None),
        check_vma=False,
    )
```

```python
import functools

import jax
import jax.numpy as jnp
import numpy as np
from jax import lax
from jax.experimental import pallas as pl
from jax.experimental.pallas import tpu as pltpu
from jax.sharding import PartitionSpec as P

HEADS = 48
KV_HEADS = 8
GROUP = HEADS // KV_HEADS
HEAD_DIM = 128
EXPERT_WINDOW = 2
LANES = 128
CHUNK = 768
PIECE = 16
MESH = pl.DeviceIdType.MESH


def rotation_tables(size):
    half = HEAD_DIM // 2
    inverse = np.float32(1000000.0) ** (-(np.arange(half, dtype=np.float32) * 2.0) / HEAD_DIM)
    angles = np.arange(size, dtype=np.float32)[:, None] * inverse.astype(np.float32)[None, :]
    cosine, sine = np.cos(angles), np.sin(angles)
    return (
        np.concatenate([cosine, cosine], axis=1).astype(np.float32),
        np.concatenate([-sine, sine], axis=1).astype(np.float32),
    )


def rotate(head, cosine, sine):
    half = HEAD_DIM // 2
    swapped = jnp.concatenate([head[:, half:], head[:, :half]], axis=1)
    return head * cosine + swapped * sine


def kernel(
    n, tok_in, attn_gain_in, w_qkv_in, w_out_in, moe_gain_in, w_gate_in, w_up_in, w_down_in,
    cos_in, sin_in, ids_in, gates_in, out,
    w_qkv, w_out, w_gate, w_up, w_down, own_tok, attn_gain, moe_gain, cos_tab, sin_tab,
    ids, gates, stage, tok_all, tok_f32, heads, att_all, gate_sum, up_sum, square_sum,
    part_f32, part_all, pair_in, pair_out, part_in,
    small_sem, weight_sem, send_sem, relay_sem, recv_sem, pair_sem, out_send, out_recv,
):
    me = lax.axis_index("tensor")
    core = lax.rem(me, 2)
    chip = me // 2
    partner = me + 1 - 2 * core
    chips = n // 2
    size = gate_sum.shape[0]
    tiles = attn_gain.shape[0]
    width = tiles * LANES
    rows = stage.shape[0] // tiles
    block = rows * tiles
    per_dev = w_qkv.shape[1] // HEAD_DIM
    chunks = width // CHUNK
    per_chunk = CHUNK // LANES
    out_cols = w_out.shape[1]
    pieces = tiles // PIECE
    share = rows * PIECE

    small = [
        pltpu.make_async_copy(src, dst, small_sem.at[i])
        for i, (src, dst) in enumerate(
            [(tok_in, own_tok), (attn_gain_in, attn_gain), (moe_gain_in, moe_gain),
             (cos_in, cos_tab), (sin_in, sin_tab), (ids_in, ids), (gates_in, gates)]
        )
    ]
    weight = [
        pltpu.make_async_copy(src, dst, weight_sem.at[i])
        for i, (src, dst) in enumerate(
            [(w_qkv_in, w_qkv), (w_out_in, w_out), (w_gate_in, w_gate), (w_up_in, w_up),
             (w_down_in, w_down)]
        )
    ]
    small[0].start()

    def chip_at(step):
        bits = [2**b for b in range(chips.bit_length() - 1)]
        return sum(lax.rem(chip // bit + step // bit, 2) * bit for bit in bits)

    chip_from = chip_at

    barrier = pltpu.get_barrier_semaphore()
    pl.semaphore_signal(barrier, inc=1, device_id={"tensor": partner}, device_id_type=MESH)

    @pl.loop(1, chips)
    def _(step):
        pl.semaphore_signal(
            barrier, inc=1, device_id={"tensor": chip_at(step) * 2 + core}, device_id_type=MESH
        )

    for copy in small[1:]:
        copy.start()
    for copy in weight:
        copy.start()
    small[0].wait()
    for tile in range(tiles):
        piece = own_tok[:, tile * LANES : (tile + 1) * LANES].astype(jnp.float32)
        for row in range(rows):
            stage[row * tiles + tile : row * tiles + tile + 1, :] = piece[row : row + 1, :]
    tok_all[me] = stage[...].astype(jnp.bfloat16)
    my_block = pl.ds(pl.multiple_of(me * block, 16), block)
    tok_f32[my_block, :] = stage[...]
    pl.semaphore_wait(barrier, chips)

    def transfer(phase, src, dst, target, send, slot):
        return pltpu.make_async_remote_copy(
            src_ref=src, dst_ref=dst, send_sem=send, recv_sem=recv_sem.at[phase, slot],
            device_id={"tensor": target}, device_id_type=MESH,
        )

    def direct(phase, ref, step):
        return transfer(
            phase, ref.at[me], ref.at[me], chip_at(step) * 2 + core, send_sem.at[phase, step], me
        )

    def relay(phase, ref, step):
        source = chip_from(step) * 2 + core
        return transfer(
            phase, ref.at[source], ref.at[source], partner, relay_sem.at[phase, step], source
        )

    def arrived(phase, ref, source):
        transfer(
            phase, ref.at[source], ref.at[source], partner, relay_sem.at[phase, 0], source
        ).wait_recv()

    def gather(phase, ref, consume):
        @pl.loop(1, chips)
        def _(step):
            direct(phase, ref, chips - step).start()

        relay(phase, ref, 0).start()
        if consume is not None:
            consume(me)

        def take_direct(step):
            source = chip_from(step) * 2 + core
            arrived(phase, ref, source)
            relay(phase, ref, step).start()
            if consume is not None:
                consume(source)

        def take_relayed(step):
            source = chip_from(step) * 2 + 1 - core
            arrived(phase, ref, source)
            if consume is not None:
                consume(source)

        lag = min(4, chips)
        pl.loop(1, lag)(take_direct)

        @pl.loop(lag, chips)
        def _(step):
            take_direct(step)
            take_relayed(step - lag)

        pl.loop(chips - lag, chips)(take_relayed)

    def gather_left(phase, ref):
        @pl.loop(0, chips)
        def _(step):
            relay(phase, ref, step).wait_send()

        @pl.loop(1, chips)
        def _(step):
            direct(phase, ref, step).wait_send()

    def widen(source):
        here = pl.ds(pl.multiple_of(source * block, 16), block)
        tok_f32[here, :] = tok_all[source].astype(jnp.float32)

    gather(0, tok_all, widen)
    for copy in small[1:]:
        copy.wait()

    def tok_tile(tile):
        return tok_f32[pl.ds(tile, size, stride=tiles), :]

    weight[0].wait()

    def project(chunk, totals):
        product, squares = totals
        pieces = []
        for i in range(per_chunk):
            tile = chunk * per_chunk + i
            value = tok_tile(tile)
            squares = squares + value * value
            pieces.append((value * attn_gain[pl.ds(tile, 1), :]).astype(jnp.bfloat16))
        here = pl.ds(pl.multiple_of(chunk * CHUNK, CHUNK), CHUNK)
        x = jnp.concatenate(pieces, axis=1)
        return product + jnp.dot(x, w_qkv[here, :], preferred_element_type=jnp.float32), squares

    product, squares = lax.fori_loop(
        0, chunks, project,
        (jnp.zeros((size, w_qkv.shape[1]), jnp.float32), jnp.zeros((size, LANES), jnp.float32)),
    )
    scale = lax.rsqrt(jnp.sum(squares, axis=1, keepdims=True) / width + 1e-05)
    columns = (product * scale).astype(jnp.bfloat16)

    turns = jnp.where(me * per_dev >= HEADS + KV_HEADS, 0.0, 1.0)
    cosine = cos_tab[...] * turns + (1.0 - turns)
    sine = sin_tab[...] * turns
    for i in range(per_dev):
        head = columns[:, i * HEAD_DIM : (i + 1) * HEAD_DIM].astype(jnp.float32)
        heads[me, i] = rotate(head, cosine, sine).astype(jnp.bfloat16)

    gather(1, heads, None)
    weight[1].wait()

    q_pos = lax.rem(lax.broadcasted_iota(jnp.int32, (GROUP * size, size), 0), size)
    k_pos = lax.broadcasted_iota(jnp.int32, (GROUP * size, size), 1)
    allowed = k_pos <= q_pos

    def head_at(index):
        return heads[index // per_dev, lax.rem(index, per_dev)]

    def attend(g, total):
        queries = jnp.concatenate([head_at(g * GROUP + i) for i in range(GROUP)], axis=0)
        scores = lax.dot_general(
            queries, head_at(HEADS + g), (((1,), (1,)), ((), ())),
            preferred_element_type=jnp.float32,
        ) * np.float32(1.0 / np.sqrt(HEAD_DIM))
        scores = jnp.where(allowed, scores, -1e30)
        top = jnp.max(scores, axis=1, keepdims=True)
        weights = jnp.where(allowed, jnp.exp(scores - top), 0.0)
        summed = jnp.dot(
            weights.astype(jnp.bfloat16), head_at(HEADS + KV_HEADS + g),
            preferred_element_type=jnp.float32,
        )
        mixed = (summed / jnp.sum(weights, axis=1, keepdims=True)).astype(jnp.bfloat16)
        mixed = jnp.concatenate([mixed[i * size : (i + 1) * size] for i in range(GROUP)], axis=1)
        depth = GROUP * HEAD_DIM
        here = pl.ds(pl.multiple_of(g * depth, depth), depth)
        return total + jnp.dot(mixed, w_out[here, :], preferred_element_type=jnp.float32)

    att_all[me] = lax.fori_loop(
        0, KV_HEADS, attend, jnp.zeros((size, out_cols), jnp.float32), unroll=8
    ).astype(jnp.bfloat16)

    gate_sum[...] = jnp.zeros_like(gate_sum)
    up_sum[...] = jnp.zeros_like(up_sum)
    square_sum[...] = jnp.zeros_like(square_sum)
    weight[2].wait()
    weight[3].wait()

    def expert_input(index, attended):
        wide = attended.shape[1]
        pieces = []
        total = square_sum[...]
        for i in range(wide // LANES):
            tile = index * (wide // LANES) + i
            here = pl.ds(tile, size, stride=tiles)
            value = tok_f32[here, :] + attended[:, i * LANES : (i + 1) * LANES]
            tok_f32[here, :] = value
            total = total + value * value
            pieces.append((value * moe_gain[pl.ds(tile, 1), :]).astype(jnp.bfloat16))
        square_sum[...] = total
        x = jnp.concatenate(pieces, axis=1)
        here = pl.ds(pl.multiple_of(index * wide, LANES), wide)
        gate_sum[...] += jnp.dot(x, w_gate[here, :], preferred_element_type=jnp.float32)
        up_sum[...] += jnp.dot(x, w_up[here, :], preferred_element_type=jnp.float32)

    if out_cols % LANES == 0:
        gather(2, att_all, lambda source: expert_input(source, att_all[source].astype(jnp.float32)))
    else:
        gather(2, att_all, None)
        joined = CHUNK // out_cols

        @pl.loop(0, chunks)
        def _(chunk):
            expert_input(chunk, jnp.concatenate(
                [att_all[chunk * joined + i].astype(jnp.float32) for i in range(joined)], axis=1
            ))

    scale = lax.rsqrt(jnp.sum(square_sum[...], axis=1, keepdims=True) / width + 1e-05)
    gate = gate_sum[...] * scale
    hidden = (gate * (1.0 / (1.0 + jnp.exp(-gate))) * (up_sum[...] * scale)).astype(jnp.bfloat16)
    weight[4].wait()

    def pair(piece):
        return pltpu.make_async_remote_copy(
            src_ref=part_all.at[piece, 1 - core], dst_ref=pair_in.at[piece],
            send_sem=pair_sem.at[0, piece], recv_sem=pair_sem.at[1, piece],
            device_id={"tensor": partner}, device_id_type=MESH,
        )

    def summed(piece, index):
        return (
            part_all[piece, core, index].astype(jnp.float32)
            + pair_in[piece, index].astype(jnp.float32)
        )

    def delivery(piece, target, slot, step):
        return pltpu.make_async_remote_copy(
            src_ref=pair_out.at[piece, target], dst_ref=part_in.at[piece, slot],
            send_sem=out_send.at[piece, step], recv_sem=out_recv.at[piece, slot],
            device_id={"tensor": target * 2 + core}, device_id_type=MESH,
        )

    strip = 4 * LANES
    for piece in range(pieces):
        for j in range(PIECE * LANES // strip):
            first = piece * PIECE * LANES + j * strip
            part = jnp.dot(
                hidden, w_down[:, first : first + strip], preferred_element_type=jnp.float32
            )
            for i in range(strip // LANES):
                part_f32[piece, pl.ds(j * (strip // LANES) + i, size, stride=PIECE), :] = part[
                    :, i * LANES : (i + 1) * LANES
                ]

        @pl.loop(0, chips, unroll=4)
        def _(index):
            for c in range(2):
                here = pl.ds(pl.multiple_of((index * 2 + c) * share, 16), share)
                part_all[piece, c, index] = part_f32[piece, here, :].astype(jnp.bfloat16)

        pair(piece).start()

    for piece in range(pieces):
        pair(piece).wait_recv()

        @pl.loop(1, chips)
        def _(step):
            target = chip_at(chips - step)
            pair_out[piece, target] = summed(piece, target).astype(jnp.bfloat16)
            delivery(piece, target, chip, chips - step).start()

        part_in[piece, chip] = summed(piece, chip).astype(jnp.bfloat16)

    picked = [
        [
            sum(jnp.where(ids[row, k] == e, gates[row, k], 0.0) for k in range(2))
            for e in range(EXPERT_WINDOW)
        ]
        for row in range(rows)
    ]
    gather_left(0, tok_all)
    gather_left(1, heads)
    gather_left(2, att_all)
    owners = chips // EXPERT_WINDOW
    for piece in range(pieces):
        pair(piece).wait_send()

        @pl.loop(1, chips)
        def _(step):
            delivery(piece, chip, chip_from(step), step).wait_recv()

        for row in range(rows):
            first = row * tiles + piece * PIECE
            total = tok_f32[pl.ds(pl.multiple_of(me * block + first, 8), PIECE), :]
            for e in range(EXPERT_WINDOW):
                expert = jnp.zeros((PIECE, LANES), jnp.float32)
                for j in range(owners):
                    expert = expert + part_in[
                        piece, e * owners + j, row * PIECE : (row + 1) * PIECE, :
                    ].astype(jnp.float32)
                total = total + picked[row][e] * expert
            stage[first : first + PIECE, :] = total

    for tile in range(tiles):
        out[:, tile * LANES : (tile + 1) * LANES] = stage[
            pl.ds(tile, rows, stride=tiles), :
        ].astype(jnp.bfloat16)

    for piece in range(pieces):
        @pl.loop(1, chips)
        def _(step):
            delivery(piece, chip_at(step), chip, step).wait_send()


def on_device(
    tokens, attn_gain, w_qkv, w_out, moe_gain, w_gate, w_up, w_down, expert_ids, gate_weights
):
    n = lax.axis_size("tensor")
    rows, width = tokens.shape
    size = rows * n
    tiles = width // LANES
    block = rows * tiles
    per_dev = w_qkv.shape[1] // HEAD_DIM
    pieces = tiles // PIECE
    share = rows * PIECE
    cosine, sine = rotation_tables(size)
    bf16, f32 = jnp.bfloat16, jnp.float32
    any_space = pl.BlockSpec(memory_space=pl.ANY)
    result = pl.pallas_call(
        functools.partial(kernel, n),
        out_shape=jax.ShapeDtypeStruct((rows, width), bf16),
        in_specs=[any_space] * 12,
        out_specs=pl.BlockSpec(memory_space=pltpu.VMEM),
        scratch_shapes=[
            pltpu.VMEM(w_qkv.shape, bf16),
            pltpu.VMEM(w_out.shape, bf16),
            pltpu.VMEM(w_gate.shape, bf16),
            pltpu.VMEM(w_up.shape, bf16),
            pltpu.VMEM(w_down.shape, bf16),
            pltpu.VMEM(tokens.shape, bf16),
            pltpu.VMEM((tiles, LANES), f32),
            pltpu.VMEM((tiles, LANES), f32),
            pltpu.VMEM((size, HEAD_DIM), f32),
            pltpu.VMEM((size, HEAD_DIM), f32),
            pltpu.SMEM(expert_ids.shape, jnp.int32),
            pltpu.SMEM(gate_weights.shape, f32),
            pltpu.VMEM((block, LANES), f32),
            pltpu.VMEM((n, block, LANES), bf16),
            pltpu.VMEM((n * block, LANES), f32),
            pltpu.VMEM((n, per_dev, size, HEAD_DIM), bf16),
            pltpu.VMEM((n, size, w_out.shape[1]), bf16),
            pltpu.VMEM((size, w_gate.shape[1]), f32),
            pltpu.VMEM((size, w_up.shape[1]), f32),
            pltpu.VMEM((size, LANES), f32),
            pltpu.VMEM((pieces, n * share, LANES), f32),
            pltpu.VMEM((pieces, 2, n // 2, share, LANES), bf16),
            pltpu.VMEM((pieces, n // 2, share, LANES), bf16),
            pltpu.VMEM((pieces, n // 2, share, LANES), bf16),
            pltpu.VMEM((pieces, n // 2, share, LANES), bf16),
            pltpu.SemaphoreType.DMA((7,)),
            pltpu.SemaphoreType.DMA((5,)),
            pltpu.SemaphoreType.DMA((3, n // 2)),
            pltpu.SemaphoreType.DMA((3, n // 2)),
            pltpu.SemaphoreType.DMA((3, n)),
            pltpu.SemaphoreType.DMA((2, pieces)),
            pltpu.SemaphoreType.DMA((pieces, n // 2)),
            pltpu.SemaphoreType.DMA((pieces, n // 2)),
        ],
        compiler_params=pltpu.CompilerParams(
            collective_id=0, has_side_effects=True, vmem_limit_bytes=56 * 1024 * 1024
        ),
        name="layer",
    )(
        tokens, attn_gain.reshape(tiles, LANES), w_qkv, w_out, moe_gain.reshape(tiles, LANES),
        w_gate, w_up, w_down, jnp.asarray(cosine), jnp.asarray(sine), expert_ids, gate_weights,
    )
    return result


def solution(mesh):
    return jax.shard_map(
        on_device,
        mesh=mesh,
        in_specs=(
            P(("groups", "tensor"), None),
            P(),
            P(None, "tensor"),
            P(None, "tensor"),
            P(),
            P(None, "tensor"),
            P(None, "tensor"),
            P("tensor", None),
            P(("groups", "tensor"), None),
            P(("groups", "tensor"), None),
        ),
        out_specs=P(("groups", "tensor"), None),
        check_vma=False,
    )
```
